32 devices in a mesh: dp: 16 (over z, y, x), fsdp: 2 (over core).
Axes of the slice: x: 2, y: 2, z: 4, core: 2. Of those that a mesh axis runs over, the one named last changes fastest.
Arguments:
- inputs: bfloat16 [12288, 8192], P('dp', 'fsdp'), may hold values from -6 to 6
- grad_out: bfloat16 [12288, 14336], P('dp', 'fsdp'), may hold values from -0.053955078 to 0.053955078
- projector: bfloat16 [8192, 256], P('fsdp', 'dp'), may hold values from -0.0625 to 0.0625
- moment: float32 [14336, 256], P(('fsdp', 'dp')), may hold values from -3 to 3
- second: float32 [14336, 256], P(('fsdp', 'dp')), may hold values from 0.05 to 2
Outputs:
- update: bfloat16 [2, 7168, 8192], P(None, 'dp', 'fsdp')
- moment_new: float32 [14336, 256], P(('fsdp', 'dp'))
- second_new: float32 [14336, 256], P(('fsdp', 'dp'))
The draws below stay inside these ranges and needn't reach their ends.
All inputs are finite; a program needn't handle non-finite values.
Results may differ from the reference program's by a relative error of at most 0.005.
Values may be sent and summed in bfloat16 or wider, within the bound.
No kernel may reach another device: no remote copies, remote signals or barrier semaphores. Data moves between devices by JAX's collectives and lax.ppermute only.
A program may use at most 64 MiB of HBM per device.

```python
import math
import jax
import jax.numpy as jnp
from jax import lax

D = 8192
FW = 14336
R = 256
STEP = 10
TOKENS = 12288
FB = 7168
N_FSDP = 2


def strengthened(drawn, key, source, target, shards_of, factor):
    def block_of(position):
        return (jnp.arange(drawn.shape[position]) // (drawn.shape[position] // shards_of)).reshape((-1,) + (1,) * (drawn.ndim - 1 - position))

    one_side = jax.random.permutation(key, shards_of)[block_of(target)]
    far = (block_of(target) + shards_of // 2) % shards_of
    return jnp.where((block_of(source) == one_side) | (block_of(source) == far), factor * drawn, drawn)


def level_of(rng, shape, split, smallest, largest):
    def one(axis_at, parts):
        heights = jax.random.uniform(jax.random.fold_in(jax.random.fold_in(rng, 6), axis_at), (parts,), jnp.float32, smallest / len(split), largest / len(split))
        return jnp.repeat(jnp.exp(heights), shape[axis_at] // parts).reshape((-1,) + (1,) * (len(shape) - axis_at - 1))

    gain = one(*split[0])
    for cut in split[1:]:
        gain = gain * one(*cut)
    return gain


def gaussian(stream_key, extent, deviation, reach, cuts=(), kind=jnp.bfloat16):
    drawn = jax.random.normal(stream_key, extent, jnp.float32) * deviation
    if len(cuts) > 0:
        drawn = level_of(stream_key, extent, cuts, -0.22, 0.18) * drawn
    return jnp.clip(drawn, min=-reach, max=reach).astype(kind)


def bell_draw_with(stream_key, extent, spread, limit, pieces, heavy, dtype=jnp.bfloat16):
    entries = spread * jax.random.normal(stream_key, extent, jnp.float32)
    if pieces:
        entries = entries * level_of(stream_key, extent, pieces, -0.22, 0.18)
    return jnp.clip(strengthened(entries, jax.random.fold_in(stream_key, 3), *heavy), -limit, limit).astype(dtype)


def setup_inputs(seed: int = 0) -> dict:
    key_of = jax.random.split(jax.random.key(seed), 6)
    return {
        "inputs": gaussian(key_of[0], (TOKENS, D), 1.0, 6.0, ((0, 16), (1, 2))),
        "grad_out": bell_draw_with(key_of[1], (TOKENS, FW), (TOKENS ** -0.5), 0.053955078, ((0, 16), (1, 2)), (0, 1, 16, 2.0)),
        "projector": gaussian(key_of[2], (D, R), D ** -0.5, 0.0625, ((0, 2), (1, 16))),
        "moment": gaussian(key_of[3], (FW, R), 0.5, 3.0, ((0, 32),), jnp.float32),
        "second": jnp.clip(jnp.exp(math.log(2.0) - 3.6888794 * jax.random.uniform(key_of[4], (FW, R), jnp.float32) ** level_of(key_of[4], (FW, R), ((0, 32),), -0.2, 0.2)), 0.05, 2.0),
    }


BETA_FIRST = 0.9
BETA_SECOND = 0.999
EPSILON = 1e-08

def adam_direction(grad_sub, moment, second):
    moment_new = BETA_FIRST * moment + (1.0 - BETA_FIRST) * grad_sub
    second_new = BETA_SECOND * second + (1.0 - BETA_SECOND) * grad_sub * grad_sub
    first_hat = moment_new / (1.0 - BETA_FIRST ** STEP)
    second_hat = second_new / (1.0 - BETA_SECOND ** STEP)
    direction = (first_hat / (jnp.sqrt(second_hat) + EPSILON)).astype(jnp.bfloat16)
    return (moment_new, second_new, direction)

def reference(inputs, grad_out, projector, moment, second):
    projected = jnp.dot(inputs, projector, preferred_element_type=jnp.float32).astype(jnp.bfloat16)
    grad_sub = lax.dot_general(grad_out, projected, (((0,), (0,)), ((), ())), preferred_element_type=jnp.float32)
    moment_new, second_new, direction = adam_direction(grad_sub, moment, second)
    decoded = lax.dot_general(direction, projector, (((1,), (1,)), ((), ())), preferred_element_type=jnp.float32)
    update = decoded.astype(jnp.bfloat16).reshape(N_FSDP, FB, D)
    return (update, moment_new, second_new)
```

```python
import functools
import math

import jax
import jax.numpy as jnp
from jax import lax
from jax.experimental import pallas as pl
from jax.experimental.pallas import tpu as pltpu
from jax.sharding import PartitionSpec as P

STEP = 10


BETA_FIRST = 0.9
BETA_SECOND = 0.999
EPSILON = 1e-08


def adam_direction(grad_sub, moment, second):
    moment_new = BETA_FIRST * moment + (1.0 - BETA_FIRST) * grad_sub
    second_new = BETA_SECOND * second + (1.0 - BETA_SECOND) * grad_sub * grad_sub
    first_hat = moment_new / (1.0 - BETA_FIRST**STEP)
    second_hat = second_new / (1.0 - BETA_SECOND**STEP)
    direction = (first_hat / (jnp.sqrt(second_hat) + EPSILON)).astype(jnp.bfloat16)
    return (moment_new, second_new, direction)


def swap(block, axis, bit):
    size = lax.axis_size(axis)
    return lax.ppermute(block, axis, [(i, i ^ (1 << bit)) for i in range(size)])


def bit_of(index, bit):
    return (index >> bit) & 1


PHASES = ((0, 1, 2), (2, 0, 1), (1, 2, 0))
CHAINS = ((0, 1, 2, 3), (1, 2, 0, 3), (2, 0, 1, 3))
GATHERS = ((3, 1, 2, 0), (3, 2, 0, 1), (3, 0, 1, 2))


def column_parts(features):
    first = round(0.34 * features / 128) * 128
    return first, features - 2 * first, first


def row_parts(owned):
    first = round(0.32 * owned / 16) * 16
    return first, first, owned - 2 * first


def share(length, unit):
    units = length // unit
    ends = [(units * (p + 1) + 1) // 3 * unit for p in range(3)]
    return ends[0], ends[1] - ends[0], length - ends[1]


def swap_all(blocks, steps):
    return lax.optimization_barrier(
        [swap(block, "dp", bit) for block, bit in zip(blocks, steps)]
    )


def joined(held, other, bit, bits):
    first = bit_of(lax.axis_index("dp"), bit) == 0
    low = jnp.where(first, held, other)
    high = jnp.where(first, other, held)
    return jnp.concatenate([low, high], axis=bits - 1 - bit)


def gather_basis(columns, bits):
    rows, features = columns.shape
    whole = columns.reshape((1,) * bits + (rows, features))
    for bit in range(bits - 1, 2, -1):
        (other,) = swap_all([whole], [bit])
        whole = joined(whole, other, bit, bits)
    parts, start = [], 0
    for length in share(features, math.gcd(features, 128)):
        parts.append(whole[..., start : start + length])
        start += length
    for steps in PHASES[::-1]:
        others = swap_all(parts, steps)
        parts = [joined(h, o, bit, bits) for h, o, bit in zip(parts, others, steps)]
    return jnp.concatenate([part.reshape(-1, part.shape[-1]) for part in parts], axis=1)


def split(total, bit, bits):
    axis = bits - 1 - bit
    mine = bit_of(lax.axis_index("dp"), bit)
    kept = lax.dynamic_slice_in_dim(total, mine, 1, axis)
    given = lax.dynamic_slice_in_dim(total, 1 - mine, 1, axis).astype(jnp.bfloat16)
    return kept, given


def halved_all(pairs, steps):
    others = swap_all([given for _, given in pairs], steps)
    return [
        kept.astype(jnp.float32) + other.astype(jnp.float32)
        for (kept, _), other in zip(pairs, others)
    ]


VMEM = pl.BlockSpec(memory_space=pltpu.VMEM)
HBM = pl.BlockSpec(memory_space=pltpu.HBM)
MIB = 1024 * 1024
LIMIT = pltpu.CompilerParams(vmem_limit_bytes=16 * MIB)
TURN_LIMITS = [pltpu.CompilerParams(vmem_limit_bytes=size * MIB) for size in (48, 44)]


def bit_here(bit):
    return bit_of(lax.axis_index("dp"), bit)


def remaining(gone, bits):
    return [bit for bit in range(bits) if bit not in gone]


def gathered_kernels(columns, bits, turn):
    lengths = column_parts(columns.shape[1])
    whole = columns.reshape((1,) + columns.shape)
    other = swap(whole, "dp", 3)
    whole, other, early = lax.optimization_barrier((own(whole), other, turn(0)))
    held = list(join([whole], [other], [0], [3], lengths))
    others, places = [None] * 3, [None] * 3
    for part, order in enumerate(GATHERS):
        have = [3]
        for number, bit in enumerate(order[1:]):
            others[part] = swap(held[part], "dp", bit)
            have = sorted(have + [bit])
            places[part] = have.index(bit)
            if number < 2:
                (held[part],) = join([held[part]], [others[part]], [places[part]], [bit], None)
    others[0], late = lax.optimization_barrier((others[0], turn(1)))
    return list(zip(held, others, places, [order[3] for order in GATHERS])), [*early, *late]


def own_kernel(block_ref, out_ref):
    out_ref[...] = block_ref[...]


def own(block):
    return pl.pallas_call(
        own_kernel,
        out_shape=jax.ShapeDtypeStruct(block.shape, block.dtype),
        in_specs=[VMEM],
        out_specs=VMEM,
        compiler_params=LIMIT,
        name="own",
    )(block)


def join_kernel(places, bits, cut, *refs):
    count = len(places)
    held, other, outs = refs[:count], refs[count : 2 * count], refs[2 * count :]
    for part, (place, bit) in enumerate(zip(places, bits)):
        mine = bit_here(bit)
        low = 1 << place
        for index in range(held[part].shape[0]):
            base = (index // low) * 2 * low + index % low
            for source, side in ((held[part], mine), (other[part], 1 - mine)):
                if cut is None:
                    outs[part][base + side * low] = source[index]
                else:
                    start = 0
                    for out, length in zip(outs, cut):
                        out[base + side * low] = source[index, :, start : start + length]
                        start += length


def join(held, others, places, bits, cut):
    shapes = [(2 * x.shape[0],) + x.shape[1:] for x in held]
    if cut:
        shapes = [shapes[0][:-1] + (length,) for length in cut]
    return pl.pallas_call(
        functools.partial(join_kernel, places, bits, cut),
        out_shape=[jax.ShapeDtypeStruct(shape, jnp.bfloat16) for shape in shapes],
        in_specs=[VMEM] * (2 * len(held)),
        out_specs=[VMEM] * len(shapes),
        compiler_params=LIMIT,
        name="join",
    )(*held, *others)


def project_kernel(steps, starts, more, last, inputs_ref, *refs):
    count = len(steps)
    ends, refs = refs[: 2 * count], refs[2 * count :]
    (total_ref, *refs) = refs if more else (None, *refs)
    bases, outs = refs[:count], refs[count:]
    total = total_ref[...] if more else None
    for part, (place, bit) in enumerate(steps):
        held, other, basis = ends[2 * part], ends[2 * part + 1], bases[part]
        mine = bit_here(bit)
        low = 1 << place
        ranks, rows, length = held.shape
        for index in range(ranks):
            base = (index // low) * 2 * low + index % low
            basis[base + mine * low] = held[index]
            basis[base + (1 - mine) * low] = other[index]
        product = lax.dot_general(
            inputs_ref[:, starts[part] : starts[part] + length],
            basis[...].reshape(2 * ranks * rows, length),
            (((1,), (1,)), ((), ())),
            preferred_element_type=jnp.float32,
        )
        total = product if total is None else total + product
    outs[0][...] = total
    if last:
        outs[1][...] = total.astype(jnp.bfloat16)


def project(inputs, ends, starts, total, last):
    tokens = inputs.shape[0]
    operands, steps, shapes = [inputs], [], []
    for held, other, place, bit in ends:
        operands += [held, other]
        steps.append((place, bit))
        ranks, rows, length = held.shape
        shapes.append(jax.ShapeDtypeStruct((2 * ranks, rows, length), jnp.bfloat16))
    more = total is not None
    shapes.append(jax.ShapeDtypeStruct((tokens, 2 * ranks * rows), jnp.float32))
    if more:
        operands.append(total)
    if last:
        shapes.append(jax.ShapeDtypeStruct((tokens, 2 * ranks * rows), jnp.bfloat16))
    return pl.pallas_call(
        functools.partial(project_kernel, steps, starts, more, last),
        out_shape=shapes,
        in_specs=[VMEM] * len(operands),
        out_specs=[VMEM] * len(shapes),
        compiler_params=LIMIT,
        name="project",
    )(*operands)


def turn_kernel(half, lengths, owned, grad_ref, *refs):
    outs, (block, sems) = refs[:3], refs[3:]
    slots = block.shape[0]
    width = 2 * owned
    steps = grad_ref.shape[1] // width // 2
    first = half * steps

    def copy(step):
        columns = slice((first + step) * width, (first + step + 1) * width)
        slot = step % slots
        return pltpu.make_async_copy(
            grad_ref.at[:, columns], block.at[slot], sems.at[slot]
        )

    for step in range(slots):
        copy(step).start()
    for step in range(steps):
        copy(step).wait()
        rows = block[step % slots].T
        quarter, y = step // 2, step % 2
        for x in range(2):
            start = x * owned
            for part, length in enumerate(lengths):
                place = 2 * x + y if part == 0 else 2 * y + x
                outs[part][4 * quarter + place] = rows[start : start + length]
                start += length
        if step + slots < steps:
            copy(step + slots).start()


def turned_rows(grad_out, lengths, owned, half):
    tokens, units = grad_out.shape
    ranks = units // owned // 2
    return pl.pallas_call(
        functools.partial(turn_kernel, half, lengths, owned),
        out_shape=[
            jax.ShapeDtypeStruct((ranks, length, tokens), jnp.bfloat16) for length in lengths
        ],
        in_specs=[HBM],
        out_specs=[VMEM] * 3,
        scratch_shapes=[
            pltpu.VMEM((3, tokens, 2 * owned), jnp.bfloat16),
            pltpu.SemaphoreType.DMA((3,)),
        ],
        compiler_params=TURN_LIMITS[half],
        cost_estimate=pl.CostEstimate(
            flops=0, bytes_accessed=2 * tokens * units, transcendentals=0
        ),
        name="turn",
    )(grad_out)


def multiply(turned, projected, outs, stays):
    def write(out, first, block):
        count, length, tokens = block.shape
        terms = jnp.dot(
            block.reshape(-1, tokens), projected[...], preferred_element_type=jnp.float32
        )
        out[first : first + count] = terms.astype(out.dtype).reshape(count, length, -1)

    for part, out in outs.items():
        side = bit_here(CHAINS[part][0])
        side = side if stays else 1 - side
        if part < 2:
            for quarter in range(4):
                place = 4 * (quarter % 2) + 2 * side
                write(out, 2 * quarter, turned[quarter // 2][part][pl.ds(place, 2)])
        else:
            for far in range(2):
                write(out, 4 * far, turned[far][part][pl.ds(4 * side, 4)])


def first_kernel(part_ref, other_ref, *refs):
    turned, out, projected = (refs[:3], refs[3:6]), refs[6], refs[7]
    total = part_ref[...] + other_ref[...].astype(jnp.float32)
    projected[...] = total.astype(jnp.bfloat16)
    multiply(turned, projected, {2: out}, False)


def terms_kernel(parts, stays, projected, *refs):
    turned, outs = (refs[:3], refs[3:6]), refs[6:]
    multiply(turned, projected, dict(zip(parts, outs)), stays)


def terms_of(turned, lengths, operands, parts, stays):
    tokens, rank = operands[-1].shape
    kind = jnp.float32 if stays else jnp.bfloat16
    shapes = [jax.ShapeDtypeStruct((8, lengths[part], rank), kind) for part in parts]
    kernel = functools.partial(terms_kernel, parts, stays)
    if len(operands) == 2:
        kernel = first_kernel
        shapes.append(jax.ShapeDtypeStruct((tokens, rank), jnp.bfloat16))
    units = 8 * sum(lengths[part] for part in parts)
    return pl.pallas_call(
        kernel,
        out_shape=shapes,
        in_specs=[VMEM] * (len(operands) + 6),
        out_specs=[VMEM] * len(shapes),
        compiler_params=LIMIT,
        cost_estimate=pl.CostEstimate(
            flops=2 * tokens * units * rank,
            bytes_accessed=2 * units * tokens,
            transcendentals=0,
        ),
        name="kept_terms" if stays else "sent_terms",
    )(*operands, *turned)


def fold_kernel(place, bit, *refs):
    count = (len(refs) - 2) // 2
    kept, got, (stay, go) = refs[:count], refs[count : 2 * count], refs[2 * count :]
    mine = bit_here(bit)
    low = 1 << place
    start = 0
    for part in range(count):
        rows = slice(start, start + kept[part].shape[1])
        for index in range(stay.shape[0]):
            base = (index // low) * 2 * low + index % low
            here = base + mine * low
            there = base + (1 - mine) * low
            stay[index, rows] = kept[part][here] + got[part][here].astype(jnp.float32)
            total = kept[part][there] + got[part][there].astype(jnp.float32)
            go[index, rows] = total.astype(jnp.bfloat16)
        start = rows.stop


def fold(kept, got, place, bit):
    ranks, _, rank = kept[0].shape
    half = (ranks // 2, sum(x.shape[1] for x in kept), rank)
    return pl.pallas_call(
        functools.partial(fold_kernel, place, bit),
        out_shape=[
            jax.ShapeDtypeStruct(half, jnp.float32),
            jax.ShapeDtypeStruct(half, jnp.bfloat16),
        ],
        in_specs=[VMEM] * (2 * len(kept)),
        out_specs=[VMEM] * 2,
        compiler_params=LIMIT,
        name="fold",
    )(*kept, *got)


def adam_kernel(start, kept_ref, got_ref, moment_ref, second_ref, first, second, way):
    rows = pl.ds(start, first.shape[0])
    grad_sub = kept_ref[...] + got_ref[...].astype(jnp.float32)
    first[...], second[...], way[...] = adam_direction(
        grad_sub.reshape(first.shape), moment_ref[rows], second_ref[rows]
    )


def adam(kept, got, moment, second, start):
    shape = kept.shape[-2:]
    return pl.pallas_call(
        functools.partial(adam_kernel, start),
        out_shape=[
            jax.ShapeDtypeStruct(shape, jnp.float32),
            jax.ShapeDtypeStruct(shape, jnp.float32),
            jax.ShapeDtypeStruct(shape, jnp.bfloat16),
        ],
        in_specs=[VMEM] * 4,
        out_specs=[VMEM] * 3,
        compiler_params=LIMIT,
        name="adam",
    )(kept, got, moment, second)


def columns_of(bases):
    pieces, start = [], 0
    for part, basis in enumerate(bases):
        length = basis.shape[1]
        for first in range(0, length, 512):
            end = min(first + 512, length)
            pieces.append((part, first, slice(start + first, start + end)))
        start += length
    return pieces


def decode_kernel(nears, start, moments, holds, *refs):
    count = len(nears)
    directions, refs = refs[:count], refs[count:]
    bases, refs = refs[:3], refs[3:]
    pieces = refs[:moments]
    outs = refs[moments + holds :][: 1 + moments]
    block, sems, moment_sems = refs[-3:]
    here = pl.ds(start, block.shape[1])
    core = lax.axis_index("fsdp")
    copies = []
    for number, piece in enumerate(pieces):
        copies.append(
            pltpu.make_async_copy(piece, outs[1 + number].at[here], moment_sems.at[number])
        )
        copies[-1].start()
    for number, near in enumerate(nears):
        side = core if near else 1 - core
        for piece, (part, first, columns) in enumerate(columns_of(bases)):
            width = columns.stop - columns.start
            decoded = jnp.dot(
                directions[number][...],
                bases[part][:, first : first + width],
                preferred_element_type=jnp.float32,
            )
            block[number, :, columns] = decoded.astype(jnp.bfloat16)
            copies.append(
                pltpu.make_async_copy(
                    block.at[number, :, columns],
                    outs[0].at[side, here, columns],
                    sems.at[number, piece],
                )
            )
            copies[-1].start()
    for copy in copies:
        copy.wait()


def decode(directions, nears, bases, start, owned, pieces, held):
    rows, rank = directions[0].shape
    features = sum(basis.shape[1] for basis in bases)
    whole = jax.ShapeDtypeStruct((owned, rank), jnp.float32)
    shapes = [jax.ShapeDtypeStruct((2, owned, features), jnp.bfloat16)]
    shapes += [whole] * len(pieces)
    count = len(directions)
    given = count + len(bases) + len(pieces)
    return pl.pallas_call(
        functools.partial(decode_kernel, nears, start, len(pieces), len(held)),
        out_shape=shapes,
        in_specs=[VMEM] * given + [HBM] * len(held),
        out_specs=[HBM] * len(shapes),
        scratch_shapes=[
            pltpu.VMEM((count, rows, features), jnp.bfloat16),
            pltpu.SemaphoreType.DMA((count, len(columns_of(bases)))),
            pltpu.SemaphoreType.DMA((2,)),
        ],
        input_output_aliases={given + i: i for i in range(len(held))},
        compiler_params=LIMIT,
        name="decode",
    )(*directions, *bases, *pieces, *held)


def exchanged(kept, got, order, number):
    bit = order[number]
    place = remaining(order[:number], len(order)).index(bit)
    stay, go = fold(kept, got, place, bit)
    return stay, swap(go, "dp", bit)


def sum_in_kernels(turned, part, other, lengths):
    last, projected = terms_of(turned, lengths, (part, other), (2,), False)
    far = swap(last, "dp", CHAINS[2][0])
    sent = terms_of(turned, lengths, (projected,), (0, 1), False)
    got = [swap(x, "dp", order[0]) for x, order in zip(sent, CHAINS)]
    got.append(far)
    kept = terms_of(turned, lengths, (projected,), (0, 1, 2), True)
    pairs = list(zip(kept, got))
    for number in range(1, 4):
        for p, order in enumerate(CHAINS):
            if p == 2 or number < 3:
                kept, got = pairs[p]
                pairs[p] = exchanged([kept], [got], order, number)
    both = exchanged(*zip(*pairs[:2]), CHAINS[0], 3)
    return both, pairs[2]


def plain_terms(grad_out, projected, lengths, owned, bits):
    terms = lax.dot_general(
        grad_out, projected, (((0,), (0,)), ((), ())), preferred_element_type=jnp.float32
    )
    terms = terms.reshape((2,) * bits + (owned, -1))
    pairs, start = [], 0
    for bit, length in enumerate(lengths):
        pairs.append(split(terms[..., start : start + length, :], bit, bits))
        start += length
    return pairs


def sum_rows(pairs, lengths, bits):
    shaped = []
    for bit, (length, pair) in enumerate(zip(lengths, pairs)):
        shape = [2] * bits
        shape[bits - 1 - bit] = 1
        shaped.append([x.reshape(tuple(shape) + (length, -1)) for x in pair])
    sums = halved_all(shaped, PHASES[0])
    for steps in PHASES[1:]:
        sums = halved_all([split(x, bit, bits) for x, bit in zip(sums, steps)], steps)
    total = jnp.concatenate(sums, axis=bits)
    for bit in range(3, bits):
        (total,) = halved_all([split(total, bit, bits)], [bit])
    return total.reshape(-1, total.shape[-1])


def exchange(block):
    return swap(block, "fsdp", 0)


def kernel_local(inputs, grad_out, projector, moment, second):
    ranks = lax.axis_size("dp")
    bits = ranks.bit_length() - 1
    owned = grad_out.shape[1] // ranks
    lengths = row_parts(owned)

    def turn(half):
        return turned_rows(grad_out, lengths, owned, half)

    ends, turned = gathered_kernels(projector.T, bits, turn)
    widths = [end[0].shape[2] for end in ends]
    starts = [0, widths[0], widths[0] + widths[1]]
    left, total = project(inputs, [ends[0]], [starts[0]], None, False)
    right, total = project(inputs, [ends[2]], [starts[2]], total, False)
    middle, part, sent = project(inputs, [ends[1]], [starts[1]], total, True)
    bases = [x.reshape(-1, x.shape[2]) for x in (left, middle, right)]
    other = exchange(sent)
    both, last = sum_in_kernels(turned, part, other, lengths)
    held = []
    start = lengths[0] + lengths[1]
    *pieces, direction = adam(*last, moment, second, start)
    far = exchange(direction)
    held = decode([direction], [True], bases, start, owned, pieces, held)
    far, held = lax.optimization_barrier((far, held))
    update, *moments = held
    (update,) = decode([far], [False], bases, start, owned, [], [update])
    held = [update, *moments]
    both, held = lax.optimization_barrier((both, held))
    *pieces, direction = adam(*both, moment, second, 0)
    far = exchange(direction)
    held = decode([direction], [True], bases, 0, owned, pieces, held)
    far, held = lax.optimization_barrier((far, held))
    update, *moments = held
    (update,) = decode([far], [False], bases, 0, owned, [], [update])
    return (update, *moments)


def plain_local(inputs, grad_out, projector, moment, second):
    ranks = lax.axis_size("dp")
    bits = ranks.bit_length() - 1
    basis = gather_basis(projector.T, bits)
    part = lax.dot_general(
        inputs, basis, (((1,), (1,)), ((), ())), preferred_element_type=jnp.float32
    )
    projected = lax.psum(part, "fsdp").astype(jnp.bfloat16)
    owned = grad_out.shape[1] // ranks
    lengths = share(owned, math.gcd(owned, 16))
    pairs = plain_terms(grad_out, projected, lengths, owned, bits)
    grad_sub = sum_rows(pairs, lengths, bits)
    moment_new, second_new, direction = adam_direction(grad_sub, moment, second)
    gathered = lax.all_gather(direction, "fsdp", axis=0, tiled=True)
    decoded = lax.dot_general(
        gathered, basis, (((1,), (0,)), ((), ())), preferred_element_type=jnp.float32
    )
    blocks = lax.axis_size("fsdp")
    update = decoded.astype(jnp.bfloat16).reshape(blocks, owned, decoded.shape[1])
    return (update, moment_new, second_new)


def local(inputs, grad_out, projector, moment, second):
    owned = grad_out.shape[1] // lax.axis_size("dp")
    fits = lax.axis_size("fsdp") == 2 and lax.axis_size("dp") == 16 and owned % 64 == 0
    run = kernel_local if fits else plain_local
    return run(inputs, grad_out, projector, moment, second)


def solution(mesh):
    return jax.shard_map(
        local,
        mesh=mesh,
        in_specs=(
            P("dp", "fsdp"),
            P("dp", "fsdp"),
            P("fsdp", "dp"),
            P(("fsdp", "dp"), None),
            P(("fsdp", "dp"), None),
        ),
        out_specs=(P(None, "dp", "fsdp"), P(("fsdp", "dp"), None), P(("fsdp", "dp"), None)),
        check_vma=False,
    )
```
